32 devices in a mesh: sr: 4 (over y, x), az: 8 (over z, core).
Axes of the slice: x: 2, y: 2, z: 4, core: 2. Of those that a mesh axis runs over, the one named last changes fastest.
Arguments:
- residual: float32 [16, 128, 10, 128], P('sr', 'az'), may hold values from -6 to 6
- dinv: float32 [16, 128, 10, 10, 128], P('sr', 'az')
- wall_jac: float32 [16, 128, 10, 10], P('sr', 'az'), may hold values from -2 to 2
- lower_coef: float32 [16, 128, 128], P('sr', 'az'), may hold values from 0.2 to 0.6
- upper_coef: float32 [16, 128, 128], P('sr', 'az'), may hold values from 0.2 to 0.6
- off_jac: float32 [4, 16, 128, 10, 10], P(None, 'sr', 'az'), may hold values from -0.7 to 0.7
- lengths: int32 [16, 128], P('sr', 'az'), may hold values from 32 to 128, as said below
- axis_flag: int32 [128], P('az'), may hold values 0 or 1
- partner: int32 [128], P('az'), may hold values from 0 to 15, as said below
Outputs:
- update: float32 [16, 128, 10, 128], P('sr', 'az')
- next_rhs: float32 [16, 128, 10, 128], P('sr', 'az')
The draws below stay inside these ranges and needn't reach their ends.
Inputs may be any that keep to these rules, and one draw needn't show every extreme that they name: `lengths`: active points of a line; some line has all 128. `partner`: within each aligned block of 16 azimuths the entries are a permutation of 0 to 15.
All inputs are finite; a program needn't handle non-finite values. No bound on the sum of `axis_flag` on one device may be relied on, other than what follows from the above.
Results may differ from the reference program's by a relative error of at most 0.0001.
Values sent between devices are 32-bit elements; how exact they have to be, the bound alone decides.
A program may use at most 64 MiB of HBM per device.

```python
import math
import jax
import jax.numpy as jnp
from jax import lax

NV = 10
NW = 128
KL = 16
INNER = 4
SWEEPS = 2
NI = 16
NAZ = 128
N_AZ = 8


def draw_dinv(key, part):
    key = jax.random.fold_in(key, 1)
    first, second = jax.random.split(key)
    diag = jnp.exp(jax.random.uniform(first, (NI, NAZ, NV, NW), jnp.float32, math.log(0.4), math.log(1.0)))
    offdiag = 0.06 * jax.random.normal(second, (NI, NAZ, NV, NV, NW), jnp.float32)
    ident = (jnp.arange(NV)[:, None] == jnp.arange(NV)[None, :]).astype(jnp.float32)
    return ident[None, None, :, :, None] * diag[:, :, :, None, :] + offdiag


def draw_lengths(key, part):
    key = jax.random.fold_in(key, 2)
    values = jax.random.randint(key, (NI, NAZ), NW // 4, NW + 1)
    return values.at[0, 0].set(NW).astype(jnp.int32)


def draw_partner(key, part):
    key = jax.random.fold_in(key, 3)
    keys = jax.random.split(key, NAZ // KL)
    perms = jax.vmap(lambda single: jax.random.permutation(single, KL))(keys)
    return perms.reshape(NAZ).astype(jnp.int32)


def set_ends(values, own_key, least, high):
    index_at = [jax.random.randint(jax.random.fold_in(own_key, axis), (), 0, length) for axis, length in enumerate(values.shape)]
    widest = values.shape.index(max(values.shape))
    neighbour = index_at[:widest] + [(index_at[widest] + 1) % values.shape[widest]] + index_at[widest + 1:]
    return values.at[tuple(index_at)].set(least).at[tuple(neighbour)].set(high)


def block_levels(rng, extent, shards, least, top_value):
    level = 1.0
    for dim, parts in shards:
        draws = jax.random.uniform(jax.random.fold_in(jax.random.fold_in(rng, 6), dim), (parts,), jnp.float32, least / len(shards), top_value / len(shards))
        level = level * jnp.repeat(jnp.exp(draws), extent[dim] // parts).reshape((-1,) + (1,) * (len(extent) - 1 - dim))
    return level


def centred(own_key, shape, width, most, cuts=(), held_as=jnp.bfloat16):
    array = width * jax.random.normal(own_key, shape, jnp.float32)
    if cuts:
        array = array * block_levels(own_key, shape, cuts, -0.22, 0.18)
    return jnp.clip(array, -most, most).astype(held_as)


def setup_inputs(seed: int = 0) -> dict:
    splits = jax.random.split(jax.random.key(seed), 10)
    return {
        "residual": centred(splits[0], (NI, NAZ, NV, NW), 1.0, 6.0, ((0, 4), (1, 8)), jnp.float32),
        "dinv": draw_dinv(jax.random.fold_in(splits[9], 71), 0),
        "wall_jac": centred(splits[2], (NI, NAZ, NV, NV), NV ** -0.5, 2.0, ((0, 4), (1, 8)), jnp.float32),
        "lower_coef": jnp.clip(0.2 + 0.400000021 * jax.random.uniform(splits[3], (NI, NAZ, NW), jnp.float32) ** block_levels(splits[3], (NI, NAZ, NW), ((0, 4), (1, 8)), -0.2, 0.2), 0.2, 0.6),
        "upper_coef": jnp.clip(0.2 + 0.400000021 * jax.random.uniform(splits[4], (NI, NAZ, NW), jnp.float32) ** block_levels(splits[4], (NI, NAZ, NW), ((0, 4), (1, 8)), -0.2, 0.2), 0.2, 0.6),
        "off_jac": centred(splits[5], (4, NI, NAZ, NV, NV), 0.12, 0.7, ((1, 4), (2, 8)), jnp.float32),
        "lengths": draw_lengths(jax.random.fold_in(splits[9], 71), 0),
        "axis_flag": set_ends((jax.random.randint(splits[7], (NAZ,), 0, 4) < 3).astype(jnp.int32), jax.random.fold_in(splits[7], 1), 0, 1),
        "partner": draw_partner(jax.random.fold_in(splits[9], 71), 0),
    }


HIGH = lax.Precision.HIGHEST


def solve_lines(rhs, dinv, wall_jac, lower_coef, upper_coef, active):
    def apply_inverse(vec):
        return jnp.einsum('...abw,...bw->...aw', dinv, vec, precision=HIGH)
    mask = active[..., None, :]
    update = apply_inverse(rhs) * mask
    for step in range(INNER):
        zeros = jnp.zeros_like(update[..., :1])
        below = jnp.concatenate([zeros, update[..., :-1]], axis=-1)
        above = jnp.concatenate([update[..., 1:], zeros], axis=-1)
        cross = lower_coef[..., None, :] * jnp.einsum('...ab,...bw->...aw', wall_jac, below, precision=HIGH)
        cross = cross + upper_coef[..., None, :] * jnp.einsum('...ba,...bw->...aw', wall_jac, above, precision=HIGH)
        update = apply_inverse(rhs - cross) * mask
    return update


def neighbour_sum(update, off_jac, axis_flag, partner):
    total_az = update.shape[1]
    azimuth = jnp.arange(total_az, dtype=jnp.int32)
    target = (((azimuth // KL) + N_AZ // 2) % N_AZ) * KL + partner
    polar = jnp.take(update[0], target, axis=0) * axis_flag.astype(jnp.float32)[:, None, None]
    below = jnp.concatenate([polar[None], update[:-1]], axis=0)
    above = jnp.concatenate([update[1:], jnp.zeros_like(update[:1])], axis=0)
    left = jnp.roll(update, 1, axis=1)
    right = jnp.roll(update, -1, axis=1)
    total = jnp.zeros_like(update)
    for direction, lines in enumerate((below, above, left, right)):
        total = total + jnp.einsum('ikab,ikbw->ikaw', off_jac[direction], lines, precision=HIGH)
    return total


def reference(residual, dinv, wall_jac, lower_coef, upper_coef, off_jac, lengths, axis_flag, partner):
    points = residual.shape[-1]
    active = (jnp.arange(points, dtype=jnp.int32)[None, None, :] < lengths[:, :, None]).astype(jnp.float32)

    def row_solve(items):
        return solve_lines(*items)

    update = jnp.zeros_like(residual)
    for sweep in range(SWEEPS):
        if sweep == 0:
            rhs = residual
        else:
            rhs = residual - neighbour_sum(update, off_jac, axis_flag, partner)
        update = lax.map(row_solve, (rhs, dinv, wall_jac, lower_coef, upper_coef, active))
    next_rhs = residual - neighbour_sum(update, off_jac, axis_flag, partner)
    return update, next_rhs
```

```python
import functools
import jax
import jax.numpy as jnp
from jax import lax
from jax.experimental import pallas as pl
from jax.experimental.pallas import tpu as pltpu
from jax.sharding import PartitionSpec as P

INNER = 4
SUB = 8
MESH = pl.DeviceIdType.MESH


def transpose_in(ref, lead, out_store, nv):
    block = ref[lead + (slice(0, SUB),)]
    turned = jnp.swapaxes(block, 0, 1)
    for b in range(SUB):
        out_store(b, turned[b])
    for b in range(SUB, nv):
        out_store(b, ref[lead + (b,)])


def kernel(sizes, res_hbm, dinv_hbm, wall_ref, low_ref, up_ref, off_ref, len_ref, pick_ref,
           upd_ref, next_ref,
           dnat, dtab, jtab, otab, rtab, rhs, lowm, upm, act, u, polar, left_out, right_out,
           left_in, right_in, rnat, load_sem, send_sem, recv_sem):
    n_sr, n_az, rows, lines, nv, points = sizes
    halves = lines // SUB
    groups = rows * halves
    sr, az = lax.axis_index("sr"), lax.axis_index("az")
    west, east = lax.rem(az + n_az - 1, n_az), lax.rem(az + 1, n_az)
    across = lax.rem(az + n_az // 2, n_az)
    last = n_sr - 1

    barrier = pltpu.get_barrier_semaphore()

    def greet(dst):
        pl.semaphore_signal(barrier, inc=1, device_id=dst, device_id_type=MESH)

    greet((sr, west))
    greet((sr, east))

    @pl.when(sr > 0)
    def _():
        greet((sr - 1, az))

    @pl.when(sr < last)
    def _():
        greet((sr + 1, az))

    @pl.when(sr == 0)
    def _():
        greet((0, across))

    def load(i):
        return pltpu.make_async_copy(dinv_hbm.at[i], dnat.at[i], load_sem.at[i])

    res_copy = pltpu.make_async_copy(res_hbm, rnat, load_sem.at[rows])
    res_copy.start()
    for i in range(rows):
        load(i).start()

    lane = lax.broadcasted_iota(jnp.int32, (SUB, points), 1)

    def place(g):
        return lax.div(g, halves), pl.multiple_of(lax.rem(g, halves) * SUB, SUB)

    @pl.when(sr == last)
    def _():
        u[0, rows + 1] = jnp.zeros(u.shape[2:], jnp.float32)
        u[1, rows + 1] = jnp.zeros(u.shape[2:], jnp.float32)

    @pl.loop(0, groups)
    def _(g):
        i, k = place(g)
        eight = pl.ds(k, SUB)
        lowm[g] = jnp.where(lane > 0, low_ref[i, eight, :], 0.0)
        upm[g] = jnp.where(lane < points - 1, up_ref[i, eight, :], 0.0)
        act[g] = (lane < len_ref[i, eight, :]).astype(jnp.float32)
        for a in range(nv):
            row = wall_ref[i, eight, a, :]
            for b in range(nv):
                jtab[g, a * nv + b] = jnp.broadcast_to(row[:, b:b + 1], (SUB, points))
        for d in range(4):
            for a in range(nv):
                otab[g, d * nv + a, :, 0:nv] = off_ref[d, i, eight, a, :]

    res_copy.wait()

    @pl.loop(0, groups)
    def _(g):
        i, k = place(g)
        for a in range(nv):
            rtab[g, a] = rnat[i, pl.ds(k, SUB), a, :]

    for i in range(rows):
        load(i).wait()

    @pl.loop(0, groups)
    def _(g):
        i, k = place(g)
        for a in range(nv):
            def put(b, value, a=a):
                dtab[g, a * nv + b] = value
            block = jnp.swapaxes(dnat[i, pl.ds(k, SUB), a, 0:SUB, :], 0, 1)
            for b in range(SUB):
                put(b, block[b])
            for b in range(SUB, nv):
                put(b, dnat[i, pl.ds(k, SUB), a, b, :])

    def inverse(g, vec):
        out = []
        for a in range(nv):
            total = dtab[g, a * nv] * vec[0]
            for b in range(1, nv):
                total = total + dtab[g, a * nv + b] * vec[b]
            out.append(total * act[g])
        return out

    def solve(slot, right_side):
        @pl.loop(0, groups)
        def _(g):
            i, k = place(g)

            def step(_, x):
                below = [lowm[g] * pltpu.roll(v, 1, 1) for v in x]
                above = [upm[g] * pltpu.roll(v, points - 1, 1) for v in x]
                cross = [right_side[g, a] for a in range(nv)]
                for b in range(nv):
                    for a in range(nv):
                        cross[a] = cross[a] - jtab[g, a * nv + b] * below[b]
                        cross[a] = cross[a] - jtab[g, b * nv + a] * above[b]
                return tuple(inverse(g, cross))

            x = tuple(inverse(g, [right_side[g, a] for a in range(nv)]))
            x = lax.fori_loop(0, INNER, step, x)
            for a in range(nv):
                u[slot, i + 1, a, pl.ds(pl.multiple_of(k + SUB, SUB), SUB), :] = x[a]

    def exchange(slot):
        for i in range(rows):
            for a in range(nv):
                left_out[slot, i, a] = u[slot, i + 1, a, SUB]
                right_out[slot, i, a] = u[slot, i + 1, a, SUB + lines - 1]

        def copy(src, dst, kind, dev):
            return pltpu.make_async_remote_copy(
                src_ref=src, dst_ref=dst, send_sem=send_sem.at[slot, kind],
                recv_sem=recv_sem.at[slot, kind], device_id=dev, device_id_type=MESH)

        mid = pl.ds(SUB, lines)
        first, final = u.at[slot, 1, :, mid], u.at[slot, rows, :, mid]
        to_west = copy(left_out.at[slot], right_in.at[slot], 0, (sr, west))
        to_east = copy(right_out.at[slot], left_in.at[slot], 1, (sr, east))
        down = copy(first, u.at[slot, rows + 1, :, mid], 2, (jnp.maximum(sr - 1, 0), az))
        upward = copy(final, u.at[slot, 0, :, mid], 3, (jnp.minimum(sr + 1, last), az))
        over = copy(first, polar.at[slot], 4, (0, across))

        @pl.when(sr == 0)
        def _():
            over.start()

        @pl.when(sr > 0)
        def _():
            down.start()

        @pl.when(sr < last)
        def _():
            upward.start()

        to_west.start()
        to_east.start()

        to_west.wait()
        to_east.wait()
        for i in range(rows):
            for a in range(nv):
                u[slot, i + 1, a, SUB - 1] = left_in[slot, i, a]
                u[slot, i + 1, a, SUB + lines] = right_in[slot, i, a]

        @pl.when(sr > 0)
        def _():
            down.wait_send()
            upward.wait_recv()

        @pl.when(sr < last)
        def _():
            upward.wait_send()
            down.wait_recv()

        @pl.when(sr == 0)
        def _():
            over.wait()
            for a in range(nv):
                u[slot, 0, a, mid] = jnp.dot(
                    pick_ref[...], polar[slot, a], precision=lax.Precision.HIGHEST,
                    preferred_element_type=jnp.float32)

    def residual_less(slot, store):
        @pl.loop(0, rows)
        def _(i):
            for half in range(halves):
                g = i * halves + half
                base = SUB + half * SUB
                acc = [rtab[g, a] for a in range(nv)]
                for d, (di, dk) in enumerate(((0, 0), (2, 0), (1, -1), (1, 1))):
                    near = [u[slot, i + di, b, base + dk:base + dk + SUB] for b in range(nv)]
                    for a in range(nv):
                        coef = otab[g, d * nv + a]
                        for b in range(nv):
                            acc[a] = acc[a] - jnp.broadcast_to(
                                coef[:, b:b + 1], (SUB, points)) * near[b]
                store(g, i, half, acc)

    def keep(g, i, half, acc):
        for a in range(nv):
            rhs[g, a] = acc[a]

    def finish(g, i, half, acc):
        for a in range(nv):
            next_ref[a, i, half * SUB:(half + 1) * SUB, :] = acc[a]

    solve(0, rtab)

    @pl.when(sr == last)
    def _():
        pl.semaphore_wait(barrier, 3)

    @pl.when(sr < last)
    def _():
        pl.semaphore_wait(barrier, 4)

    exchange(0)
    residual_less(0, keep)
    solve(1, rhs)
    exchange(1)
    for i in range(rows):
        for a in range(nv):
            upd_ref[a, i] = u[1, i + 1, a, SUB:SUB + lines, :]
    residual_less(1, finish)


def body(mesh_sizes, residual, dinv, wall_jac, lower_coef, upper_coef, off_jac, lengths, axis_flag, partner):
    rows, lines, nv, points = residual.shape
    n_sr, n_az = mesh_sizes
    groups = rows * (lines // SUB)
    sizes = (n_sr, n_az, rows, lines, nv, points)
    pick = jnp.where(
        partner[:, None] == lax.broadcasted_iota(jnp.int32, (lines, lines), 1),
        axis_flag[:, None].astype(jnp.float32), 0.0)
    vmem = pl.BlockSpec(memory_space=pltpu.VMEM)
    hbm = pl.BlockSpec(memory_space=pl.ANY)
    out = jax.ShapeDtypeStruct((nv, rows, lines, points), jnp.float32)
    f32 = jnp.float32
    update, next_rhs = pl.pallas_call(
        functools.partial(kernel, sizes),
        out_shape=(out, out),
        in_specs=[hbm, hbm, vmem, vmem, vmem, vmem, vmem, vmem],
        out_specs=(vmem, vmem),
        scratch_shapes=[
            pltpu.VMEM((rows, lines, nv, nv, points), f32),
            pltpu.VMEM((groups, nv * nv, SUB, points), f32),
            pltpu.VMEM((groups, nv * nv, SUB, points), f32),
            pltpu.VMEM((groups, 4 * nv, SUB, 128), f32),
            pltpu.VMEM((groups, nv, SUB, points), f32),
            pltpu.VMEM((groups, nv, SUB, points), f32),
            pltpu.VMEM((groups, SUB, points), f32),
            pltpu.VMEM((groups, SUB, points), f32),
            pltpu.VMEM((groups, SUB, points), f32),
            pltpu.VMEM((2, rows + 2, nv, lines + 2 * SUB, points), f32),
            pltpu.VMEM((2, nv, lines, points), f32),
            pltpu.VMEM((2, rows, nv, points), f32),
            pltpu.VMEM((2, rows, nv, points), f32),
            pltpu.VMEM((2, rows, nv, points), f32),
            pltpu.VMEM((2, rows, nv, points), f32),
            pltpu.VMEM((rows, lines, nv, points), f32),
            pltpu.SemaphoreType.DMA((rows + 1,)),
            pltpu.SemaphoreType.DMA((2, 5)),
            pltpu.SemaphoreType.DMA((2, 5)),
        ],
        compiler_params=pltpu.CompilerParams(
            collective_id=0, has_side_effects=True, vmem_limit_bytes=48 * 2**20),
    )(residual, dinv, wall_jac, lower_coef, upper_coef, off_jac, lengths[:, :, None], pick)
    back = (1, 2, 0, 3)
    return update.transpose(back), next_rhs.transpose(back)


def solution(mesh):
    in_specs = (
        P("sr", "az", None, None),
        P("sr", "az", None, None, None),
        P("sr", "az", None, None),
        P("sr", "az", None),
        P("sr", "az", None),
        P(None, "sr", "az", None, None),
        P("sr", "az"),
        P("az"),
        P("az"),
    )
    out_specs = (P("sr", "az", None, None), P("sr", "az", None, None))
    sizes = (mesh.shape["sr"], mesh.shape["az"])
    return jax.shard_map(functools.partial(body, sizes), mesh=mesh, in_specs=in_specs,
                         out_specs=out_specs, check_vma=False)
```

```python
import functools
import jax
import jax.numpy as jnp
from jax import lax
from jax.experimental import pallas as pl
from jax.experimental.pallas import tpu as pltpu
from jax.sharding import PartitionSpec as P

INNER = 4
SUB = 8
MESH = pl.DeviceIdType.MESH


def kernel(sizes, res, dinv_hbm, wall_ref, low_ref, up_ref, off_ref, len_ref, flag_ref, partner_ref,
           upd_ref, next_ref,
           dinv, jtab, flat, coef, rhs, lowm, upm, act, u, polar, left_out, right_out,
           left_in, right_in, load_sem, send_sem, recv_sem):
    n_sr, n_az, rows, lines, nv, points = sizes
    halves = lines // SUB
    groups = rows * halves
    sr, az = lax.axis_index("sr"), lax.axis_index("az")
    west, east = lax.rem(az + n_az - 1, n_az), lax.rem(az + 1, n_az)
    across = lax.rem(az + n_az // 2, n_az)
    last = n_sr - 1

    barrier = pltpu.get_barrier_semaphore()

    def greet(dst):
        pl.semaphore_signal(barrier, inc=1, device_id=dst, device_id_type=MESH)

    greet((sr, west))
    greet((sr, east))

    @pl.when(sr > 0)
    def _():
        greet((sr - 1, az))

    @pl.when(sr < last)
    def _():
        greet((sr + 1, az))

    @pl.when(sr == 0)
    def _():
        greet((0, across))

    def load(i):
        return pltpu.make_async_copy(dinv_hbm.at[i], dinv.at[i], load_sem.at[i])

    for i in range(rows):
        load(i).start()

    lane = lax.broadcasted_iota(jnp.int32, (SUB, points), 1)

    @pl.when(sr == last)
    def _():
        u[0, rows + 1] = jnp.zeros(u.shape[2:], jnp.float32)
        u[1, rows + 1] = jnp.zeros(u.shape[2:], jnp.float32)

    for i in range(rows):
        spot = slice(i * lines, (i + 1) * lines)
        for a in range(nv):
            entries = slice(a * nv, (a + 1) * nv)
            for d in range(4):
                flat[d, entries, spot] = off_ref[d, a, :, i, :]
            flat[4, entries, spot] = wall_ref[a, :, i, :]
        flat[4, nv * nv:nv * nv + 1, spot] = len_ref[i:i + 1, :].astype(jnp.float32)
    flat[4, nv * nv + 1:nv * nv + 2, 0:lines] = partner_ref[...].astype(jnp.float32)
    flat[4, nv * nv + 2:nv * nv + 3, 0:lines] = flag_ref[...].astype(jnp.float32)
    for d in range(5):
        coef[d] = jnp.transpose(flat[d])
    pick = jnp.where(
        coef[4, 0:lines, nv * nv + 1:nv * nv + 2]
        == lax.broadcasted_iota(jnp.int32, (lines, lines), 1).astype(jnp.float32),
        coef[4, 0:lines, nv * nv + 2:nv * nv + 3], 0.0)

    @pl.loop(0, groups)
    def _(g):
        i = lax.div(g, halves)
        eight = pl.ds(pl.multiple_of(lax.rem(g, halves) * SUB, SUB), SUB)
        lowm[g] = jnp.where(lane > 0, low_ref[i, eight, :], 0.0)
        upm[g] = jnp.where(lane < points - 1, up_ref[i, eight, :], 0.0)
        own = coef[4, pl.ds(pl.multiple_of(g * SUB, SUB), SUB), :]
        length = own[:, nv * nv:nv * nv + 1]
        act[g] = (lane.astype(jnp.float32) < length).astype(jnp.float32)
        for entry in range(nv * nv):
            jtab[g, entry] = jnp.broadcast_to(own[:, entry:entry + 1], (SUB, points))

    def inverse(i, half, vec):
        g = i * halves + half
        eight = slice(half * SUB, (half + 1) * SUB)
        out = [dinv[i, a, 0, eight, :] * vec[0] for a in range(nv)]
        for b in range(1, nv):
            for a in range(nv):
                out[a] = out[a] + dinv[i, a, b, eight, :] * vec[b]
        return [v * act[g] for v in out]

    def solve(slot, right_side):
        @pl.loop(0, rows)
        def _(i):
            if slot == 0:
                load(i).wait()

            def right(half):
                return [right_side[i, a, half * SUB:(half + 1) * SUB, :] for a in range(nv)]

            def step(_, xs):
                news = []
                for half in range(halves):
                    g = i * halves + half
                    x = xs[half]
                    below = [lowm[g] * pltpu.roll(v, 1, 1) for v in x]
                    above = [upm[g] * pltpu.roll(v, points - 1, 1) for v in x]
                    cross = right(half)
                    for b in range(nv):
                        for a in range(nv):
                            entry = jtab[g, a * nv + b]
                            cross[a] = cross[a] - entry * below[b]
                            cross[b] = cross[b] - entry * above[a]
                    news.append(tuple(inverse(i, half, cross)))
                return tuple(news)

            xs = tuple(tuple(inverse(i, half, right(half))) for half in range(halves))
            xs = lax.fori_loop(0, INNER, step, xs)
            for half in range(halves):
                base = SUB + half * SUB
                for a in range(nv):
                    u[slot, i + 1, a, base:base + SUB, :] = xs[half][a]
            for a in range(nv):
                left_out[slot, i, a] = xs[0][a][0]
                right_out[slot, i, a] = xs[halves - 1][a][SUB - 1]
            if slot == 1:
                for half in range(halves):
                    for a in range(nv):
                        upd_ref[i, a, half * SUB:(half + 1) * SUB, :] = xs[half][a]

    def exchange(slot):
        def copy(src, dst, kind, dev):
            return pltpu.make_async_remote_copy(
                src_ref=src, dst_ref=dst, send_sem=send_sem.at[slot, kind],
                recv_sem=recv_sem.at[slot, kind], device_id=dev, device_id_type=MESH)

        mid = pl.ds(SUB, lines)
        first, final = u.at[slot, 1, :, mid], u.at[slot, rows, :, mid]
        to_west = copy(left_out.at[slot], right_in.at[slot], 0, (sr, west))
        to_east = copy(right_out.at[slot], left_in.at[slot], 1, (sr, east))
        down = copy(first, u.at[slot, rows + 1, :, mid], 2, (jnp.maximum(sr - 1, 0), az))
        upward = copy(final, u.at[slot, 0, :, mid], 3, (jnp.minimum(sr + 1, last), az))
        over = copy(first, polar.at[slot], 4, (0, across))

        @pl.when(sr == 0)
        def _():
            over.start()

        @pl.when(sr > 0)
        def _():
            down.start()

        @pl.when(sr < last)
        def _():
            upward.start()

        to_west.start()
        to_east.start()

        to_west.wait()
        to_east.wait()
        for i in range(rows):
            for a in range(nv):
                u[slot, i + 1, a, SUB - 1] = left_in[slot, i, a]
                u[slot, i + 1, a, SUB + lines] = right_in[slot, i, a]

        @pl.when(sr > 0)
        def _():
            down.wait_send()
            upward.wait_recv()

        @pl.when(sr < last)
        def _():
            upward.wait_send()
            down.wait_recv()

        @pl.when(sr == 0)
        def _():
            over.wait()
            wide = jnp.concatenate([polar[slot, a] for a in range(nv)], axis=1)
            moved = jnp.dot(pick, wide, precision=lax.Precision.HIGHEST,
                            preferred_element_type=jnp.float32)
            for a in range(nv):
                u[slot, 0, a, mid] = moved[:, a * points:(a + 1) * points]

    def residual_less(slot, out):
        @pl.loop(0, rows)
        def _(i):
            for half in range(halves):
                g = i * halves + half
                base = SUB + half * SUB
                acc = [res[i, a, half * SUB:(half + 1) * SUB, :] for a in range(nv)]
                for d, (di, dk) in enumerate(((0, 0), (2, 0), (1, -1), (1, 1))):
                    near = [u[slot, i + di, b, base + dk:base + dk + SUB] for b in range(nv)]
                    own = coef[d, pl.ds(pl.multiple_of(g * SUB, SUB), SUB), :]
                    for b in range(nv):
                        for a in range(nv):
                            entry = own[:, a * nv + b:a * nv + b + 1]
                            acc[a] = acc[a] - jnp.broadcast_to(entry, (SUB, points)) * near[b]
                for a in range(nv):
                    out[i, a, half * SUB:(half + 1) * SUB, :] = acc[a]

    solve(0, res)

    @pl.when(sr == last)
    def _():
        pl.semaphore_wait(barrier, 3)

    @pl.when(sr < last)
    def _():
        pl.semaphore_wait(barrier, 4)

    exchange(0)
    residual_less(0, rhs)
    solve(1, rhs)
    exchange(1)
    residual_less(1, next_ref)


def body(mesh_sizes, residual, dinv, wall_jac, lower_coef, upper_coef, off_jac, lengths, axis_flag, partner):
    rows, lines, nv, points = residual.shape
    n_sr, n_az = mesh_sizes
    groups = rows * (lines // SUB)
    sizes = (n_sr, n_az, rows, lines, nv, points)
    vmem = pl.BlockSpec(memory_space=pltpu.VMEM)
    hbm = pl.BlockSpec(memory_space=pl.ANY)
    out = jax.ShapeDtypeStruct((rows, nv, lines, points), jnp.float32)
    f32 = jnp.float32
    update, next_rhs = pl.pallas_call(
        functools.partial(kernel, sizes),
        out_shape=(out, out),
        in_specs=[vmem, hbm] + [vmem] * 7,
        out_specs=(vmem, vmem),
        scratch_shapes=[
            pltpu.VMEM((rows, nv, nv, lines, points), f32),
            pltpu.VMEM((groups, nv * nv, SUB, points), f32),
            pltpu.VMEM((5, 128, 128), f32),
            pltpu.VMEM((5, 128, 128), f32),
            pltpu.VMEM((rows, nv, lines, points), f32),
            pltpu.VMEM((groups, SUB, points), f32),
            pltpu.VMEM((groups, SUB, points), f32),
            pltpu.VMEM((groups, SUB, points), f32),
            pltpu.VMEM((2, rows + 2, nv, lines + 2 * SUB, points), f32),
            pltpu.VMEM((2, nv, lines, points), f32),
            pltpu.VMEM((2, rows, nv, points), f32),
            pltpu.VMEM((2, rows, nv, points), f32),
            pltpu.VMEM((2, rows, nv, points), f32),
            pltpu.VMEM((2, rows, nv, points), f32),
            pltpu.SemaphoreType.DMA((rows,)),
            pltpu.SemaphoreType.DMA((2, 5)),
            pltpu.SemaphoreType.DMA((2, 5)),
        ],
        compiler_params=pltpu.CompilerParams(
            collective_id=0, has_side_effects=True, vmem_limit_bytes=48 * 2**20),
    )(residual.transpose(0, 2, 1, 3), dinv.transpose(0, 2, 3, 1, 4), wall_jac.transpose(2, 3, 0, 1),
      lower_coef, upper_coef, off_jac.transpose(0, 3, 4, 1, 2), lengths,
      axis_flag.reshape(1, lines), partner.reshape(1, lines))
    back = (0, 2, 1, 3)
    return update.transpose(back), next_rhs.transpose(back)


def solution(mesh):
    in_specs = (
        P("sr", "az", None, None),
        P("sr", "az", None, None, None),
        P("sr", "az", None, None),
        P("sr", "az", None),
        P("sr", "az", None),
        P(None, "sr", "az", None, None),
        P("sr", "az"),
        P("az"),
        P("az"),
    )
    out_specs = (P("sr", "az", None, None), P("sr", "az", None, None))
    sizes = (mesh.shape["sr"], mesh.shape["az"])
    return jax.shard_map(functools.partial(body, sizes), mesh=mesh, in_specs=in_specs,
                         out_specs=out_specs, check_vma=False)
```

```python
import functools
import jax
import jax.numpy as jnp
from jax import lax
from jax.experimental import pallas as pl
from jax.experimental.pallas import tpu as pltpu
from jax.sharding import PartitionSpec as P

INNER = 4
SUB = 8
MESH = pl.DeviceIdType.MESH


def kernel(sizes, res_hbm, dinv_hbm, wall_hbm, low_hbm, up_hbm, off_hbm, len_hbm, flag_hbm, partner_hbm,
           upd_ref, next_ref,
           dinv, jtab, flat, coef, wide_off, rhs, lowm, upm, act, u, polar, left_out, right_out,
           left_in, right_in, res, wall_ref, low_ref, up_ref, off_ref, len_ref, flag_ref, partner_ref,
           load_sem, send_sem, recv_sem):
    n_sr, n_az, rows, lines, nv, points = sizes
    halves = lines // SUB
    groups = rows * halves
    sr, az = lax.axis_index("sr"), lax.axis_index("az")
    west, east = lax.rem(az + n_az - 1, n_az), lax.rem(az + 1, n_az)
    across = lax.rem(az + n_az // 2, n_az)
    last = n_sr - 1

    barrier = pltpu.get_barrier_semaphore()

    def greet(dst):
        pl.semaphore_signal(barrier, inc=1, device_id=dst, device_id_type=MESH)

    greet((sr, west))
    greet((sr, east))

    @pl.when(sr > 0)
    def _():
        greet((sr - 1, az))

    @pl.when(sr < last)
    def _():
        greet((sr + 1, az))

    @pl.when(sr == 0)
    def _():
        greet((0, across))

    def load(i):
        return pltpu.make_async_copy(dinv_hbm.at[i], dinv.at[i], load_sem.at[i])

    small = [pltpu.make_async_copy(src, dst, load_sem.at[rows + at]) for at, (src, dst) in enumerate((
        (off_hbm, off_ref), (wall_hbm, wall_ref), (len_hbm, len_ref), (flag_hbm, flag_ref),
        (partner_hbm, partner_ref), (low_hbm, low_ref), (up_hbm, up_ref), (res_hbm, res)))]
    for copy in small:
        copy.start()
    for i in range(rows):
        load(i).start()

    lane = lax.broadcasted_iota(jnp.int32, (SUB, points), 1)

    @pl.when(sr == last)
    def _():
        u[0, rows + 1] = jnp.zeros(u.shape[2:], jnp.float32)
        u[1, rows + 1] = jnp.zeros(u.shape[2:], jnp.float32)

    for copy in small:
        copy.wait()

    for i in range(rows):
        spot = slice(i * lines, (i + 1) * lines)
        for a in range(nv):
            entries = slice(a * nv, (a + 1) * nv)
            flat[entries, spot] = wall_ref[a, :, i, :]
        flat[nv * nv:nv * nv + 1, spot] = len_ref[i:i + 1, :].astype(jnp.float32)
    flat[nv * nv + 1:nv * nv + 2, 0:lines] = partner_ref[...].astype(jnp.float32)
    flat[nv * nv + 2:nv * nv + 3, 0:lines] = flag_ref[...].astype(jnp.float32)
    coef[...] = jnp.transpose(flat[...])
    for i in range(rows):
        for half in range(halves):
            for d in range(4):
                for b in range(nv):
                    at = (d * nv + b) * SUB
                    wide_off[i * halves + half, :, at:at + SUB] = off_ref[
                        d, :, b, i, half * SUB:(half + 1) * SUB]
    pick = jnp.where(
        coef[0:lines, nv * nv + 1:nv * nv + 2]
        == lax.broadcasted_iota(jnp.int32, (lines, lines), 1).astype(jnp.float32),
        coef[0:lines, nv * nv + 2:nv * nv + 3], 0.0)

    @pl.loop(0, groups)
    def _(g):
        i = lax.div(g, halves)
        eight = pl.ds(pl.multiple_of(lax.rem(g, halves) * SUB, SUB), SUB)
        lowm[g] = jnp.where(lane > 0, low_ref[i, eight, :], 0.0)
        upm[g] = jnp.where(lane < points - 1, up_ref[i, eight, :], 0.0)
        own = coef[pl.ds(pl.multiple_of(g * SUB, SUB), SUB), :]
        length = own[:, nv * nv:nv * nv + 1]
        act[g] = (lane.astype(jnp.float32) < length).astype(jnp.float32)
        for entry in range(nv * nv):
            jtab[g, entry] = jnp.broadcast_to(own[:, entry:entry + 1], (SUB, points))

    def inverse(i, half, vec):
        g = i * halves + half
        eight = slice(half * SUB, (half + 1) * SUB)
        out = [dinv[i, a, 0, eight, :] * vec[0] for a in range(nv)]
        for b in range(1, nv):
            for a in range(nv):
                out[a] = out[a] + dinv[i, a, b, eight, :] * vec[b]
        return [v * act[g] for v in out]

    def solve(slot, right_side):
        @pl.loop(0, rows)
        def _(i):
            if slot == 0:
                load(i).wait()

            def right(half):
                return [right_side[i, a, half * SUB:(half + 1) * SUB, :] for a in range(nv)]

            def step(half, _, x):
                if True:
                    g = i * halves + half
                    below = [lowm[g] * pltpu.roll(v, 1, 1) for v in x]
                    above = [upm[g] * pltpu.roll(v, points - 1, 1) for v in x]
                    cross = right(half)
                    for b in range(nv):
                        for a in range(nv):
                            entry = jtab[g, a * nv + b]
                            cross[a] = cross[a] - entry * below[b]
                            cross[b] = cross[b] - entry * above[a]
                    return tuple(inverse(i, half, cross))

            xs = []
            for half in range(halves):
                x = tuple(inverse(i, half, right(half)))
                xs.append(lax.fori_loop(0, INNER, functools.partial(step, half), x, unroll=True))
            for half in range(halves):
                base = SUB + half * SUB
                for a in range(nv):
                    u[slot, i + 1, a, base:base + SUB, :] = xs[half][a]
            for a in range(nv):
                left_out[slot, i, a] = xs[0][a][0]
                right_out[slot, i, a] = xs[halves - 1][a][SUB - 1]
            if slot == 1:
                for half in range(halves):
                    for a in range(nv):
                        upd_ref[i, a, half * SUB:(half + 1) * SUB, :] = xs[half][a]

    def exchange(slot):
        def copy(src, dst, kind, dev):
            return pltpu.make_async_remote_copy(
                src_ref=src, dst_ref=dst, send_sem=send_sem.at[slot, kind],
                recv_sem=recv_sem.at[slot, kind], device_id=dev, device_id_type=MESH)

        mid = pl.ds(SUB, lines)
        first, final = u.at[slot, 1, :, mid], u.at[slot, rows, :, mid]
        to_west = copy(left_out.at[slot], right_in.at[slot], 0, (sr, west))
        to_east = copy(right_out.at[slot], left_in.at[slot], 1, (sr, east))
        down = copy(first, u.at[slot, rows + 1, :, mid], 2, (jnp.maximum(sr - 1, 0), az))
        upward = copy(final, u.at[slot, 0, :, mid], 3, (jnp.minimum(sr + 1, last), az))
        over = copy(first, polar.at[slot], 4, (0, across))

        @pl.when(sr == 0)
        def _():
            over.start()

        @pl.when(sr > 0)
        def _():
            down.start()

        @pl.when(sr < last)
        def _():
            upward.start()

        to_west.start()
        to_east.start()

        to_west.wait()
        to_east.wait()
        for i in range(rows):
            for a in range(nv):
                u[slot, i + 1, a, SUB - 1] = left_in[slot, i, a]
                u[slot, i + 1, a, SUB + lines] = right_in[slot, i, a]

        @pl.when(sr > 0)
        def _():
            down.wait_send()
            upward.wait_recv()

        @pl.when(sr < last)
        def _():
            upward.wait_send()
            down.wait_recv()

        @pl.when(sr == 0)
        def _():
            over.wait()
            wide = jnp.concatenate([polar[slot, a] for a in range(nv)], axis=1)
            moved = jnp.dot(pick, wide, precision=lax.Precision.HIGHEST,
                            preferred_element_type=jnp.float32)
            for a in range(nv):
                u[slot, 0, a, mid] = moved[:, a * points:(a + 1) * points]

    span = 4 * nv * SUB
    same_line = (lax.broadcasted_iota(jnp.int32, (SUB, span), 0)
                 == lax.rem(lax.broadcasted_iota(jnp.int32, (SUB, span), 1), SUB))

    def residual_less(slot, out):
        @pl.loop(0, rows)
        def _(i):
            for half in range(halves):
                g = i * halves + half
                base = SUB + half * SUB
                near = [u[slot, i + di, b, base + dk:base + dk + SUB]
                        for di, dk in ((0, 0), (2, 0), (1, -1), (1, 1)) for b in range(nv)]
                weights = [jnp.where(same_line, jnp.broadcast_to(wide_off[g, a:a + 1, :], (SUB, span)), 0.0)
                           for a in range(nv)]
                total = jnp.dot(jnp.concatenate(weights, axis=0), jnp.concatenate(near, axis=0),
                                precision=lax.Precision.HIGHEST, preferred_element_type=jnp.float32)
                for a in range(nv):
                    rows_at = slice(half * SUB, (half + 1) * SUB)
                    out[i, a, rows_at, :] = res[i, a, rows_at, :] - total[a * SUB:(a + 1) * SUB]

    solve(0, res)

    @pl.when(sr == last)
    def _():
        pl.semaphore_wait(barrier, 3)

    @pl.when(sr < last)
    def _():
        pl.semaphore_wait(barrier, 4)

    exchange(0)
    residual_less(0, rhs)
    solve(1, rhs)
    exchange(1)
    residual_less(1, next_ref)


def body(mesh_sizes, residual, dinv, wall_jac, lower_coef, upper_coef, off_jac, lengths, axis_flag, partner):
    rows, lines, nv, points = residual.shape
    n_sr, n_az = mesh_sizes
    groups = rows * (lines // SUB)
    sizes = (n_sr, n_az, rows, lines, nv, points)
    vmem = pl.BlockSpec(memory_space=pltpu.VMEM)
    hbm = pl.BlockSpec(memory_space=pl.ANY)
    out = jax.ShapeDtypeStruct((rows, nv, lines, points), jnp.float32)
    f32 = jnp.float32
    update, next_rhs = pl.pallas_call(
        functools.partial(kernel, sizes),
        out_shape=(out, out),
        in_specs=[hbm] * 9,
        out_specs=(vmem, vmem),
        scratch_shapes=[
            pltpu.VMEM((rows, nv, nv, lines, points), f32),
            pltpu.VMEM((groups, nv * nv, SUB, points), f32),
            pltpu.VMEM((128, 128), f32),
            pltpu.VMEM((128, 128), f32),
            pltpu.VMEM((groups, nv, 4 * nv * SUB), f32),
            pltpu.VMEM((rows, nv, lines, points), f32),
            pltpu.VMEM((groups, SUB, points), f32),
            pltpu.VMEM((groups, SUB, points), f32),
            pltpu.VMEM((groups, SUB, points), f32),
            pltpu.VMEM((2, rows + 2, nv, lines + 2 * SUB, points), f32),
            pltpu.VMEM((2, nv, lines, points), f32),
            pltpu.VMEM((2, rows, nv, points), f32),
            pltpu.VMEM((2, rows, nv, points), f32),
            pltpu.VMEM((2, rows, nv, points), f32),
            pltpu.VMEM((2, rows, nv, points), f32),
            pltpu.VMEM((rows, nv, lines, points), f32),
            pltpu.VMEM((nv, nv, rows, lines), f32),
            pltpu.VMEM((rows, lines, points), f32),
            pltpu.VMEM((rows, lines, points), f32),
            pltpu.VMEM((4, nv, nv, rows, lines), f32),
            pltpu.VMEM((rows, lines), jnp.int32),
            pltpu.VMEM((1, lines), jnp.int32),
            pltpu.VMEM((1, lines), jnp.int32),
            pltpu.SemaphoreType.DMA((rows + 8,)),
            pltpu.SemaphoreType.DMA((2, 5)),
            pltpu.SemaphoreType.DMA((2, 5)),
        ],
        compiler_params=pltpu.CompilerParams(
            collective_id=0, has_side_effects=True, vmem_limit_bytes=64 * 2**20),
    )(residual.transpose(0, 2, 1, 3), dinv.transpose(0, 2, 3, 1, 4), wall_jac.transpose(2, 3, 0, 1),
      lower_coef, upper_coef, off_jac.transpose(0, 3, 4, 1, 2), lengths,
      axis_flag.reshape(1, lines), partner.reshape(1, lines))
    back = (0, 2, 1, 3)
    return update.transpose(back), next_rhs.transpose(back)


def solution(mesh):
    in_specs = (
        P("sr", "az", None, None),
        P("sr", "az", None, None, None),
        P("sr", "az", None, None),
        P("sr", "az", None),
        P("sr", "az", None),
        P(None, "sr", "az", None, None),
        P("sr", "az"),
        P("az"),
        P("az"),
    )
    out_specs = (P("sr", "az", None, None), P("sr", "az", None, None))
    sizes = (mesh.shape["sr"], mesh.shape["az"])
    return jax.shard_map(functools.partial(body, sizes), mesh=mesh, in_specs=in_specs,
                         out_specs=out_specs, check_vma=False)
```

```python
import functools
import jax
import jax.numpy as jnp
from jax import lax
from jax.experimental import pallas as pl
from jax.experimental.pallas import tpu as pltpu
from jax.sharding import PartitionSpec as P

INNER = 4
SUB = 8
MESH = pl.DeviceIdType.MESH


def kernel(sizes, res_hbm, dinv_hbm, wall_hbm, low_hbm, up_hbm, off_hbm, len_hbm, flag_hbm, partner_hbm,
           upd_ref, next_ref,
           dinv, jtab, flat, coef, wide_off, rhs, lowm, upm, act, u, polar, left_out, right_out,
           left_in, right_in, res, wall_ref, low_ref, up_ref, off_ref, len_ref, flag_ref, partner_ref,
           load_sem, send_sem, recv_sem):
    n_sr, n_az, rows, lines, nv, points = sizes
    halves = lines // SUB
    groups = rows * halves
    sr, az = lax.axis_index("sr"), lax.axis_index("az")
    west, east = lax.rem(az + n_az - 1, n_az), lax.rem(az + 1, n_az)
    across = lax.rem(az + n_az // 2, n_az)
    last = n_sr - 1

    barrier = pltpu.get_barrier_semaphore()

    def greet(dst):
        pl.semaphore_signal(barrier, inc=1, device_id=dst, device_id_type=MESH)

    greet((sr, west))
    greet((sr, east))

    @pl.when(sr > 0)
    def _():
        greet((sr - 1, az))

    @pl.when(sr < last)
    def _():
        greet((sr + 1, az))

    @pl.when(sr == 0)
    def _():
        greet((0, across))

    def load(i):
        return pltpu.make_async_copy(dinv_hbm.at[i], dinv.at[i], load_sem.at[i])

    small = [pltpu.make_async_copy(src, dst, load_sem.at[rows + at]) for at, (src, dst) in enumerate((
        (off_hbm, off_ref), (wall_hbm, wall_ref), (len_hbm, len_ref), (flag_hbm, flag_ref),
        (partner_hbm, partner_ref), (low_hbm, low_ref), (up_hbm, up_ref), (res_hbm, res)))]
    for copy in small:
        copy.start()
    for j in range(rows):
        load(j * (rows - 1) % rows).start()

    lane = lax.broadcasted_iota(jnp.int32, (SUB, points), 1)

    @pl.when(sr == last)
    def _():
        u[0, rows + 1] = jnp.zeros(u.shape[2:], jnp.float32)
        u[1, rows + 1] = jnp.zeros(u.shape[2:], jnp.float32)

    for copy in small:
        copy.wait()

    for i in range(rows):
        spot = slice(i * lines, (i + 1) * lines)
        for a in range(nv):
            entries = slice(a * nv, (a + 1) * nv)
            flat[entries, spot] = wall_ref[a, :, i, :]
        flat[nv * nv:nv * nv + 1, spot] = len_ref[i:i + 1, :].astype(jnp.float32)
    flat[nv * nv + 1:nv * nv + 2, 0:lines] = partner_ref[...].astype(jnp.float32)
    flat[nv * nv + 2:nv * nv + 3, 0:lines] = flag_ref[...].astype(jnp.float32)
    coef[...] = jnp.transpose(flat[...])
    for i in range(rows):
        for half in range(halves):
            for d in range(4):
                for b in range(nv):
                    at = (d * nv + b) * SUB
                    wide_off[i * halves + half, :, at:at + SUB] = off_ref[
                        d, :, b, i, half * SUB:(half + 1) * SUB]
    pick = jnp.where(
        coef[0:lines, nv * nv + 1:nv * nv + 2]
        == lax.broadcasted_iota(jnp.int32, (lines, lines), 1).astype(jnp.float32),
        coef[0:lines, nv * nv + 2:nv * nv + 3], 0.0)

    @pl.loop(0, groups)
    def _(g):
        i = lax.div(g, halves)
        eight = pl.ds(pl.multiple_of(lax.rem(g, halves) * SUB, SUB), SUB)
        lowm[g] = jnp.where(lane > 0, low_ref[i, eight, :], 0.0)
        upm[g] = jnp.where(lane < points - 1, up_ref[i, eight, :], 0.0)
        own = coef[pl.ds(pl.multiple_of(g * SUB, SUB), SUB), :]
        length = own[:, nv * nv:nv * nv + 1]
        act[g] = (lane.astype(jnp.float32) < length).astype(jnp.float32)
        for entry in range(nv * nv):
            jtab[g, entry] = jnp.broadcast_to(own[:, entry:entry + 1], (SUB, points))

    def inverse(i, half, vec):
        g = i * halves + half
        eight = slice(half * SUB, (half + 1) * SUB)
        out = [dinv[i, a, 0, eight, :] * vec[0] for a in range(nv)]
        for b in range(1, nv):
            for a in range(nv):
                out[a] = out[a] + dinv[i, a, b, eight, :] * vec[b]
        return [v * act[g] for v in out]

    mid = pl.ds(SUB, lines)

    def copy(slot, src, dst, kind, dev):
        return pltpu.make_async_remote_copy(
            src_ref=src, dst_ref=dst, send_sem=send_sem.at[slot, kind],
            recv_sem=recv_sem.at[slot, kind], device_id=dev, device_id_type=MESH)

    def to_west(slot, i):
        return copy(slot, left_out.at[slot, i], right_in.at[slot, i], 3 + i, (sr, west))

    def to_east(slot, i):
        return copy(slot, right_out.at[slot, i], left_in.at[slot, i], 3 + rows + i, (sr, east))

    def down(slot):
        return copy(slot, u.at[slot, 1, :, mid], u.at[slot, rows + 1, :, mid], 0,
                    (jnp.maximum(sr - 1, 0), az))

    def upward(slot):
        return copy(slot, u.at[slot, rows, :, mid], u.at[slot, 0, :, mid], 1,
                    (jnp.minimum(sr + 1, last), az))

    def over(slot):
        return copy(slot, u.at[slot, 1, :, mid], polar.at[slot], 2, (0, across))

    def send(slot, i):
        @pl.when(jnp.logical_and(i == 0, sr == 0))
        def _():
            over(slot).start()

        @pl.when(jnp.logical_and(i == 0, sr > 0))
        def _():
            down(slot).start()

        @pl.when(jnp.logical_and(i == rows - 1, sr < last))
        def _():
            upward(slot).start()

        to_west(slot, i).start()
        to_east(slot, i).start()

    def receive(slot, i):
        to_west(slot, i).wait()
        to_east(slot, i).wait()
        for a in range(nv):
            u[slot, i + 1, a, SUB - 1] = left_in[slot, i, a]
            u[slot, i + 1, a, SUB + lines] = right_in[slot, i, a]

        @pl.when(jnp.logical_and(i == 0, sr > 0))
        def _():
            down(slot).wait_send()
            upward(slot).wait_recv()

        @pl.when(jnp.logical_and(i == rows - 1, sr < last))
        def _():
            upward(slot).wait_send()
            down(slot).wait_recv()

        @pl.when(jnp.logical_and(i == 0, sr == 0))
        def _():
            over(slot).wait()
            wide = jnp.concatenate([polar[slot, a] for a in range(nv)], axis=1)
            moved = jnp.dot(pick, wide, precision=lax.Precision.HIGHEST,
                            preferred_element_type=jnp.float32)
            for a in range(nv):
                u[slot, 0, a, mid] = moved[:, a * points:(a + 1) * points]

    def solve(slot, right_side):
        @pl.loop(0, rows)
        def _(j):
            i = lax.rem(j * (rows - 1), rows)
            if slot == 0:
                load(i).wait()

            def right(half):
                return [right_side[i, a, half * SUB:(half + 1) * SUB, :] for a in range(nv)]

            def step(half, _, x):
                if True:
                    g = i * halves + half
                    below = [lowm[g] * pltpu.roll(v, 1, 1) for v in x]
                    above = [upm[g] * pltpu.roll(v, points - 1, 1) for v in x]
                    cross = right(half)
                    for b in range(nv):
                        for a in range(nv):
                            entry = jtab[g, a * nv + b]
                            cross[a] = cross[a] - entry * below[b]
                            cross[b] = cross[b] - entry * above[a]
                    return tuple(inverse(i, half, cross))

            xs = []
            for half in range(halves):
                x = tuple(inverse(i, half, right(half)))
                xs.append(lax.fori_loop(0, INNER, functools.partial(step, half), x, unroll=True))
            for half in range(halves):
                base = SUB + half * SUB
                for a in range(nv):
                    u[slot, i + 1, a, base:base + SUB, :] = xs[half][a]
            for a in range(nv):
                left_out[slot, i, a] = xs[0][a][0]
                right_out[slot, i, a] = xs[halves - 1][a][SUB - 1]
            send(slot, i)
            if slot == 1:
                for half in range(halves):
                    for a in range(nv):
                        upd_ref[i, a, half * SUB:(half + 1) * SUB, :] = xs[half][a]

    span = 4 * nv * SUB
    same_line = (lax.broadcasted_iota(jnp.int32, (SUB, span), 0)
                 == lax.rem(lax.broadcasted_iota(jnp.int32, (SUB, span), 1), SUB))

    def residual_less(slot, out):
        @pl.loop(0, rows)
        def _(j):
            i = lax.rem(j * (rows - 1), rows)
            receive(slot, i)
            for half in range(halves):
                g = i * halves + half
                base = SUB + half * SUB
                near = [u[slot, i + di, b, base + dk:base + dk + SUB]
                        for di, dk in ((0, 0), (2, 0), (1, -1), (1, 1)) for b in range(nv)]
                weights = [jnp.where(same_line, jnp.broadcast_to(wide_off[g, a:a + 1, :], (SUB, span)), 0.0)
                           for a in range(nv)]
                total = jnp.dot(jnp.concatenate(weights, axis=0), jnp.concatenate(near, axis=0),
                                precision=lax.Precision.HIGHEST, preferred_element_type=jnp.float32)
                for a in range(nv):
                    rows_at = slice(half * SUB, (half + 1) * SUB)
                    out[i, a, rows_at, :] = res[i, a, rows_at, :] - total[a * SUB:(a + 1) * SUB]

    @pl.when(sr == last)
    def _():
        pl.semaphore_wait(barrier, 3)

    @pl.when(sr < last)
    def _():
        pl.semaphore_wait(barrier, 4)

    solve(0, res)
    residual_less(0, rhs)
    solve(1, rhs)
    residual_less(1, next_ref)


def body(mesh_sizes, residual, dinv, wall_jac, lower_coef, upper_coef, off_jac, lengths, axis_flag, partner):
    rows, lines, nv, points = residual.shape
    n_sr, n_az = mesh_sizes
    groups = rows * (lines // SUB)
    sizes = (n_sr, n_az, rows, lines, nv, points)
    vmem = pl.BlockSpec(memory_space=pltpu.VMEM)
    hbm = pl.BlockSpec(memory_space=pl.ANY)
    out = jax.ShapeDtypeStruct((rows, nv, lines, points), jnp.float32)
    f32 = jnp.float32
    update, next_rhs = pl.pallas_call(
        functools.partial(kernel, sizes),
        out_shape=(out, out),
        in_specs=[hbm] * 9,
        out_specs=(vmem, vmem),
        scratch_shapes=[
            pltpu.VMEM((rows, nv, nv, lines, points), f32),
            pltpu.VMEM((groups, nv * nv, SUB, points), f32),
            pltpu.VMEM((128, 128), f32),
            pltpu.VMEM((128, 128), f32),
            pltpu.VMEM((groups, nv, 4 * nv * SUB), f32),
            pltpu.VMEM((rows, nv, lines, points), f32),
            pltpu.VMEM((groups, SUB, points), f32),
            pltpu.VMEM((groups, SUB, points), f32),
            pltpu.VMEM((groups, SUB, points), f32),
            pltpu.VMEM((2, rows + 2, nv, lines + 2 * SUB, points), f32),
            pltpu.VMEM((2, nv, lines, points), f32),
            pltpu.VMEM((2, rows, nv, points), f32),
            pltpu.VMEM((2, rows, nv, points), f32),
            pltpu.VMEM((2, rows, nv, points), f32),
            pltpu.VMEM((2, rows, nv, points), f32),
            pltpu.VMEM((rows, nv, lines, points), f32),
            pltpu.VMEM((nv, nv, rows, lines), f32),
            pltpu.VMEM((rows, lines, points), f32),
            pltpu.VMEM((rows, lines, points), f32),
            pltpu.VMEM((4, nv, nv, rows, lines), f32),
            pltpu.VMEM((rows, lines), jnp.int32),
            pltpu.VMEM((1, lines), jnp.int32),
            pltpu.VMEM((1, lines), jnp.int32),
            pltpu.SemaphoreType.DMA((rows + 8,)),
            pltpu.SemaphoreType.DMA((2, 3 + 2 * rows)),
            pltpu.SemaphoreType.DMA((2, 3 + 2 * rows)),
        ],
        compiler_params=pltpu.CompilerParams(
            collective_id=0, has_side_effects=True, vmem_limit_bytes=64 * 2**20),
    )(residual.transpose(0, 2, 1, 3), dinv.transpose(0, 2, 3, 1, 4), wall_jac.transpose(2, 3, 0, 1),
      lower_coef, upper_coef, off_jac.transpose(0, 3, 4, 1, 2), lengths,
      axis_flag.reshape(1, lines), partner.reshape(1, lines))
    back = (0, 2, 1, 3)
    return update.transpose(back), next_rhs.transpose(back)


def solution(mesh):
    in_specs = (
        P("sr", "az", None, None),
        P("sr", "az", None, None, None),
        P("sr", "az", None, None),
        P("sr", "az", None),
        P("sr", "az", None),
        P(None, "sr", "az", None, None),
        P("sr", "az"),
        P("az"),
        P("az"),
    )
    out_specs = (P("sr", "az", None, None), P("sr", "az", None, None))
    sizes = (mesh.shape["sr"], mesh.shape["az"])
    return jax.shard_map(functools.partial(body, sizes), mesh=mesh, in_specs=in_specs,
                         out_specs=out_specs, check_vma=False)
```

```python
import functools
import jax
import jax.numpy as jnp
from jax import lax
from jax.experimental import pallas as pl
from jax.experimental.pallas import tpu as pltpu
from jax.sharding import PartitionSpec as P

INNER = 4
SUB = 8
MESH = pl.DeviceIdType.MESH


def kernel(sizes, res_hbm, dinv_hbm, wall_hbm, low_hbm, up_hbm, off_hbm, len_hbm, flag_hbm, partner_hbm,
           upd_ref, next_ref,
           dinv, jtab, flat, coef, wide_off, rhs, lowm, upm, act, u, polar, left_out, right_out,
           left_in, right_in, res, wall_ref, low_ref, up_ref, off_ref, len_ref, flag_ref, partner_ref,
           load_sem, send_sem, recv_sem):
    n_sr, n_az, rows, lines, nv, points = sizes
    halves = lines // SUB
    groups = rows * halves
    sr, az = lax.axis_index("sr"), lax.axis_index("az")
    west, east = lax.rem(az + n_az - 1, n_az), lax.rem(az + 1, n_az)
    across = lax.rem(az + n_az // 2, n_az)
    last = n_sr - 1

    barrier = pltpu.get_barrier_semaphore()

    def greet(dst):
        pl.semaphore_signal(barrier, inc=1, device_id=dst, device_id_type=MESH)

    greet((sr, west))
    greet((sr, east))

    @pl.when(sr > 0)
    def _():
        greet((sr - 1, az))

    @pl.when(sr < last)
    def _():
        greet((sr + 1, az))

    @pl.when(sr == 0)
    def _():
        greet((0, across))

    def load(i):
        return pltpu.make_async_copy(dinv_hbm.at[i], dinv.at[i], load_sem.at[i])

    small = [pltpu.make_async_copy(src, dst, load_sem.at[rows + at]) for at, (src, dst) in enumerate((
        (off_hbm, off_ref), (wall_hbm, wall_ref), (len_hbm, len_ref), (flag_hbm, flag_ref),
        (partner_hbm, partner_ref), (low_hbm, low_ref), (up_hbm, up_ref), (res_hbm, res)))]
    for copy in small:
        copy.start()
    for j in range(rows):
        load(j * (rows - 1) % rows).start()

    lane = lax.broadcasted_iota(jnp.int32, (SUB, points), 1)

    @pl.when(sr == last)
    def _():
        u[0, rows + 1] = jnp.zeros(u.shape[2:], jnp.float32)
        u[1, rows + 1] = jnp.zeros(u.shape[2:], jnp.float32)

    for copy in small[1:]:
        copy.wait()

    for i in range(rows):
        spot = slice(i * lines, (i + 1) * lines)
        for a in range(nv):
            entries = slice(a * nv, (a + 1) * nv)
            flat[entries, spot] = wall_ref[a, :, i, :]
        flat[nv * nv:nv * nv + 1, spot] = len_ref[i:i + 1, :].astype(jnp.float32)
    flat[nv * nv + 1:nv * nv + 2, 0:lines] = partner_ref[...].astype(jnp.float32)
    flat[nv * nv + 2:nv * nv + 3, 0:lines] = flag_ref[...].astype(jnp.float32)
    coef[...] = jnp.transpose(flat[...])
    pick = jnp.where(
        coef[0:lines, nv * nv + 1:nv * nv + 2]
        == lax.broadcasted_iota(jnp.int32, (lines, lines), 1).astype(jnp.float32),
        coef[0:lines, nv * nv + 2:nv * nv + 3], 0.0)

    @pl.loop(0, groups)
    def _(g):
        i = lax.div(g, halves)
        eight = pl.ds(pl.multiple_of(lax.rem(g, halves) * SUB, SUB), SUB)
        lowm[g] = jnp.where(lane > 0, low_ref[i, eight, :], 0.0)
        upm[g] = jnp.where(lane < points - 1, up_ref[i, eight, :], 0.0)
        own = coef[pl.ds(pl.multiple_of(g * SUB, SUB), SUB), :]
        length = own[:, nv * nv:nv * nv + 1]
        act[g] = (lane.astype(jnp.float32) < length).astype(jnp.float32)
        for entry in range(nv * nv):
            jtab[g, entry] = jnp.broadcast_to(own[:, entry:entry + 1], (SUB, points))

    def inverse(i, half, vec):
        g = i * halves + half
        eight = slice(half * SUB, (half + 1) * SUB)
        out = [dinv[i, a, 0, eight, :] * vec[0] for a in range(nv)]
        for b in range(1, nv):
            for a in range(nv):
                out[a] = out[a] + dinv[i, a, b, eight, :] * vec[b]
        return [v * act[g] for v in out]

    mid = pl.ds(SUB, lines)

    def copy(slot, src, dst, kind, dev):
        return pltpu.make_async_remote_copy(
            src_ref=src, dst_ref=dst, send_sem=send_sem.at[slot, kind],
            recv_sem=recv_sem.at[slot, kind], device_id=dev, device_id_type=MESH)

    def to_west(slot, i):
        return copy(slot, left_out.at[slot, i], right_in.at[slot, i], 3 + i, (sr, west))

    def to_east(slot, i):
        return copy(slot, right_out.at[slot, i], left_in.at[slot, i], 3 + rows + i, (sr, east))

    def down(slot):
        return copy(slot, u.at[slot, 1, :, mid], u.at[slot, rows + 1, :, mid], 0,
                    (jnp.maximum(sr - 1, 0), az))

    def upward(slot):
        return copy(slot, u.at[slot, rows, :, mid], u.at[slot, 0, :, mid], 1,
                    (jnp.minimum(sr + 1, last), az))

    def over(slot):
        return copy(slot, u.at[slot, 1, :, mid], polar.at[slot], 2, (0, across))

    def send(slot, i):
        @pl.when(jnp.logical_and(i == 0, sr == 0))
        def _():
            over(slot).start()

        @pl.when(jnp.logical_and(i == 0, sr > 0))
        def _():
            down(slot).start()

        @pl.when(jnp.logical_and(i == rows - 1, sr < last))
        def _():
            upward(slot).start()

        to_west(slot, i).start()
        to_east(slot, i).start()

    def receive(slot, i):
        to_west(slot, i).wait()
        to_east(slot, i).wait()
        for a in range(nv):
            u[slot, i + 1, a, SUB - 1] = left_in[slot, i, a]
            u[slot, i + 1, a, SUB + lines] = right_in[slot, i, a]

        @pl.when(jnp.logical_and(i == 0, sr > 0))
        def _():
            down(slot).wait_send()
            upward(slot).wait_recv()

        @pl.when(jnp.logical_and(i == rows - 1, sr < last))
        def _():
            upward(slot).wait_send()
            down(slot).wait_recv()

        @pl.when(jnp.logical_and(i == 0, sr == 0))
        def _():
            over(slot).wait()
            wide = jnp.concatenate([polar[slot, a] for a in range(nv)], axis=1)
            moved = jnp.dot(pick, wide, precision=lax.Precision.HIGHEST,
                            preferred_element_type=jnp.float32)
            for a in range(nv):
                u[slot, 0, a, mid] = moved[:, a * points:(a + 1) * points]

    def solve(slot, right_side):
        @pl.loop(0, rows)
        def _(j):
            i = lax.rem(j * (rows - 1), rows)
            if slot == 0:
                load(i).wait()

            def right(half):
                return [right_side[i, a, half * SUB:(half + 1) * SUB, :] for a in range(nv)]

            def step(half, _, x):
                if True:
                    g = i * halves + half
                    below = [lowm[g] * pltpu.roll(v, 1, 1) for v in x]
                    above = [upm[g] * pltpu.roll(v, points - 1, 1) for v in x]
                    cross = right(half)
                    for b in range(nv):
                        for a in range(nv):
                            entry = jtab[g, a * nv + b]
                            cross[a] = cross[a] - entry * below[b]
                            cross[b] = cross[b] - entry * above[a]
                    return tuple(inverse(i, half, cross))

            xs = []
            for half in range(halves):
                x = tuple(inverse(i, half, right(half)))
                xs.append(lax.fori_loop(0, INNER, functools.partial(step, half), x, unroll=True))
            for half in range(halves):
                base = SUB + half * SUB
                for a in range(nv):
                    u[slot, i + 1, a, base:base + SUB, :] = xs[half][a]
            for a in range(nv):
                left_out[slot, i, a] = xs[0][a][0]
                right_out[slot, i, a] = xs[halves - 1][a][SUB - 1]
            send(slot, i)
            if slot == 1:
                for half in range(halves):
                    for a in range(nv):
                        upd_ref[i, a, half * SUB:(half + 1) * SUB, :] = xs[half][a]

    span = 4 * nv * SUB
    same_line = (lax.broadcasted_iota(jnp.int32, (SUB, span), 0)
                 == lax.rem(lax.broadcasted_iota(jnp.int32, (SUB, span), 1), SUB))

    def residual_less(slot, out):
        @pl.loop(0, rows)
        def _(j):
            i = lax.rem(j * (rows - 1), rows)
            receive(slot, i)
            for half in range(halves):
                g = i * halves + half
                base = SUB + half * SUB
                near = [u[slot, i + di, b, base + dk:base + dk + SUB]
                        for di, dk in ((0, 0), (2, 0), (1, -1), (1, 1)) for b in range(nv)]
                weights = [jnp.where(same_line, jnp.broadcast_to(wide_off[g, a:a + 1, :], (SUB, span)), 0.0)
                           for a in range(nv)]
                total = jnp.dot(jnp.concatenate(weights, axis=0), jnp.concatenate(near, axis=0),
                                precision=lax.Precision.HIGHEST, preferred_element_type=jnp.float32)
                for a in range(nv):
                    rows_at = slice(half * SUB, (half + 1) * SUB)
                    out[i, a, rows_at, :] = res[i, a, rows_at, :] - total[a * SUB:(a + 1) * SUB]

    @pl.when(sr == last)
    def _():
        pl.semaphore_wait(barrier, 3)

    @pl.when(sr < last)
    def _():
        pl.semaphore_wait(barrier, 4)

    solve(0, res)
    small[0].wait()
    for i in range(rows):
        for half in range(halves):
            for d in range(4):
                for b in range(nv):
                    at = (d * nv + b) * SUB
                    wide_off[i * halves + half, :, at:at + SUB] = off_ref[
                        d, :, b, i, half * SUB:(half + 1) * SUB]
    residual_less(0, rhs)
    solve(1, rhs)
    residual_less(1, next_ref)


def body(mesh_sizes, residual, dinv, wall_jac, lower_coef, upper_coef, off_jac, lengths, axis_flag, partner):
    rows, lines, nv, points = residual.shape
    n_sr, n_az = mesh_sizes
    groups = rows * (lines // SUB)
    sizes = (n_sr, n_az, rows, lines, nv, points)
    vmem = pl.BlockSpec(memory_space=pltpu.VMEM)
    hbm = pl.BlockSpec(memory_space=pl.ANY)
    out = jax.ShapeDtypeStruct((rows, nv, lines, points), jnp.float32)
    f32 = jnp.float32
    update, next_rhs = pl.pallas_call(
        functools.partial(kernel, sizes),
        out_shape=(out, out),
        in_specs=[hbm] * 9,
        out_specs=(vmem, vmem),
        scratch_shapes=[
            pltpu.VMEM((rows, nv, nv, lines, points), f32),
            pltpu.VMEM((groups, nv * nv, SUB, points), f32),
            pltpu.VMEM((128, 128), f32),
            pltpu.VMEM((128, 128), f32),
            pltpu.VMEM((groups, nv, 4 * nv * SUB), f32),
            pltpu.VMEM((rows, nv, lines, points), f32),
            pltpu.VMEM((groups, SUB, points), f32),
            pltpu.VMEM((groups, SUB, points), f32),
            pltpu.VMEM((groups, SUB, points), f32),
            pltpu.VMEM((2, rows + 2, nv, lines + 2 * SUB, points), f32),
            pltpu.VMEM((2, nv, lines, points), f32),
            pltpu.VMEM((2, rows, nv, points), f32),
            pltpu.VMEM((2, rows, nv, points), f32),
            pltpu.VMEM((2, rows, nv, points), f32),
            pltpu.VMEM((2, rows, nv, points), f32),
            pltpu.VMEM((rows, nv, lines, points), f32),
            pltpu.VMEM((nv, nv, rows, lines), f32),
            pltpu.VMEM((rows, lines, points), f32),
            pltpu.VMEM((rows, lines, points), f32),
            pltpu.VMEM((4, nv, nv, rows, lines), f32),
            pltpu.VMEM((rows, lines), jnp.int32),
            pltpu.VMEM((1, lines), jnp.int32),
            pltpu.VMEM((1, lines), jnp.int32),
            pltpu.SemaphoreType.DMA((rows + 8,)),
            pltpu.SemaphoreType.DMA((2, 3 + 2 * rows)),
            pltpu.SemaphoreType.DMA((2, 3 + 2 * rows)),
        ],
        compiler_params=pltpu.CompilerParams(
            collective_id=0, has_side_effects=True, vmem_limit_bytes=64 * 2**20),
    )(residual.transpose(0, 2, 1, 3), dinv.transpose(0, 2, 3, 1, 4), wall_jac.transpose(2, 3, 0, 1),
      lower_coef, upper_coef, off_jac.transpose(0, 3, 4, 1, 2), lengths,
      axis_flag.reshape(1, lines), partner.reshape(1, lines))
    back = (0, 2, 1, 3)
    return update.transpose(back), next_rhs.transpose(back)


def solution(mesh):
    in_specs = (
        P("sr", "az", None, None),
        P("sr", "az", None, None, None),
        P("sr", "az", None, None),
        P("sr", "az", None),
        P("sr", "az", None),
        P(None, "sr", "az", None, None),
        P("sr", "az"),
        P("az"),
        P("az"),
    )
    out_specs = (P("sr", "az", None, None), P("sr", "az", None, None))
    sizes = (mesh.shape["sr"], mesh.shape["az"])
    return jax.shard_map(functools.partial(body, sizes), mesh=mesh, in_specs=in_specs,
                         out_specs=out_specs, check_vma=False)
```
